32 devices in a mesh: parts: 2 (over y), grp: 4 (over z), band: 2 (over x), half: 2 (over core).
Axes of the slice: x: 2, y: 2, z: 4, core: 2. Of those that a mesh axis runs over, the one named last changes fastest.
Arguments:
- pair_list: int32 [64, 2], P(('parts', 'grp', 'half')), parts along dimension 0, may hold values from 0 to 127, as said below
- kernel: bfloat16 [64, 1024, 1024], P(('parts', 'grp', 'half')), parts along dimension 0, may hold values from 7.785857e-07 to 0.0078125
- facet_areas: float32 [256, 1024], P(('parts', 'grp')), parts along dimension 0, may hold values from 0.5 to 2
- heat_load: float32 [256, 1024], P(('parts', 'grp')), parts along dimension 0, may hold values from 0.2 to 2
- start_t4: float32 [256, 1024], P(('parts', 'grp')), parts along dimension 0, may hold values from 0.5 to 2
- material: int32 [256, 1024], P(('parts', 'grp')), parts along dimension 0, may hold values from 0 to 7
- coating: int32 [256], P(('parts', 'grp')), parts along dimension 0, may hold values from 0 to 3
- emis_table: float32 [4, 8], replicated, may hold values from 0.2 to 0.9
- share_table: float32 [8, 8], replicated, may hold values from 0.05 to 0.3
Outputs:
- radiosity: bfloat16 [256, 8, 1024], P(('parts', 'grp'), 'band'), parts along dimension 0
- temperature: float32 [256, 1024], P(('parts', 'grp')), parts along dimension 0
The draws below stay inside these ranges and needn't reach their ends.
There are 2 independent parts, one for each index of `parts`. The reference program is written for one: setup_inputs(seed, part) draws one part's arguments, and reference() takes and returns one part's arrays. A program takes and returns all parts, laid end to end along the dimension named above; an argument that names none is the same for every part. Nothing has to cross between parts.
Inputs may be any that keep to these rules, and one draw needn't show every extreme that they name: `pair_list`: each row holds two group numbers, the first below the second.
All inputs are finite; a program needn't handle non-finite values.
Results may differ from the reference program's by a relative error of at most 0.0017.
Values may be sent and summed in bfloat16 or wider, within the bound.
A program may use at most 64 MiB of HBM per device.

```python
import math
import jax
import jax.numpy as jnp
from jax import lax

FG = 1024
NB = 8
SWEEPS = 2
NCLS = 4
NMAT = 8
G = 128
NPAIRS = 32


def draw_pair_list(key, part):
    key = jax.random.fold_in(key, 11)
    key_first, key_second = jax.random.split(key)
    first = jax.random.randint(key_first, (NPAIRS,), 0, G - 1, dtype=jnp.int32)
    second = jax.random.randint(key_second, (NPAIRS,), first + 1, G, dtype=jnp.int32)
    first = first.at[0].set(0)
    second = second.at[0].set(G - 1)
    return jnp.stack([first, second], axis=1).astype(jnp.int32)


def with_ends(result, key, smallest, high):
    extent = result.shape
    index_at = [jax.random.randint(jax.random.fold_in(key, axis), (), 0, extent[axis]) for axis in range(len(extent))]
    result = result.at[tuple(index_at)].set(smallest)
    longest = extent.index(max(extent))
    index_at[longest] = (index_at[longest] + 1) % extent[longest]
    return result.at[tuple(index_at)].set(high)


def shard_levels(rng, extent, cuts, least, top_value):
    loudness, own = 1.0, jax.random.fold_in(rng, 6)
    for axis_at, shards_of in cuts:
        draws = jnp.exp(jax.random.uniform(jax.random.fold_in(own, axis_at), (shards_of,), jnp.float32, least / len(cuts), top_value / len(cuts)))
        loudness = loudness * jnp.repeat(draws, extent[axis_at] // shards_of).reshape([-1 if axis == axis_at else 1 for axis in range(len(extent))])
    return loudness


def setup_inputs(seed: int = 0, part: int = 0) -> dict:
    arg_keys = jax.random.split(jax.random.key(seed), 10)
    part_splits = jax.random.split(jax.random.fold_in(arg_keys[9], part), 10)
    return {
        "pair_list": draw_pair_list(jax.random.fold_in(jax.random.fold_in(arg_keys[9], part), 71), part),
        "kernel": jnp.clip(jnp.exp(math.log(0.0078125) - 9.213757 * jax.random.uniform(part_splits[1], (NPAIRS, FG, FG), jnp.float32) ** shard_levels(part_splits[1], (NPAIRS, FG, FG), ((0, 8),), -0.2, 0.2)), 7.7858567237854e-07, 0.0078125).astype(jnp.bfloat16),
        "facet_areas": jnp.clip(jnp.exp(math.log(2.0) - 1.3862944 * jax.random.uniform(part_splits[2], (G, FG), jnp.float32) ** shard_levels(part_splits[2], (G, FG), ((0, 4),), -0.2, 0.2)), 0.5, 2.0),
        "heat_load": jnp.clip(jnp.exp(math.log(2.0) - 2.3025851 * jax.random.uniform(part_splits[3], (G, FG), jnp.float32) ** shard_levels(part_splits[3], (G, FG), ((0, 4),), -0.2, 0.2)), 0.2, 2.0),
        "start_t4": jnp.clip(jnp.exp(math.log(2.0) - 1.3862944 * jax.random.uniform(part_splits[4], (G, FG), jnp.float32) ** shard_levels(part_splits[4], (G, FG), ((0, 4),), -0.2, 0.2)), 0.5, 2.0),
        "material": with_ends(jax.random.randint(part_splits[5], (G, FG), 0, NMAT), jax.random.fold_in(part_splits[5], 1), 0, NMAT - 1).astype(jnp.int32),
        "coating": with_ends(jax.random.randint(part_splits[6], (G,), 0, NCLS), jax.random.fold_in(part_splits[6], 1), 0, NCLS - 1).astype(jnp.int32),
        "emis_table": jnp.clip(jax.random.uniform(arg_keys[7], (NCLS, NB), jnp.float32, 0.2, 0.9), 0.2, 0.9),
        "share_table": jnp.clip(jnp.exp(jax.random.uniform(arg_keys[8], (NMAT, NB), jnp.float32, math.log(0.05), math.log(0.3))), 0.05, 0.3),
    }


def reference(pair_list, kernel, facet_areas, heat_load, start_t4, material, coating, emis_table, share_table):
    emissivity = emis_table[coating]
    share_all = jnp.transpose(share_table[material], (0, 2, 1))
    weight_all = emissivity[:, :, None] * share_all
    emit_sum = jnp.sum(weight_all, axis=1)
    radiosity = (weight_all * start_t4[:, None, :]).astype(jnp.bfloat16)
    fourth = start_t4
    for sweep in range(SWEEPS):
        current = radiosity

        def add_pair(incoming, item):
            block, couple = item
            to_first = jnp.dot(current[couple[1]], block.T, preferred_element_type=jnp.float32)
            to_second = jnp.dot(current[couple[0]], block, preferred_element_type=jnp.float32)
            incoming = incoming.at[couple[0]].add(to_first)
            incoming = incoming.at[couple[1]].add(to_second)
            return incoming, None

        incoming, unused = lax.scan(add_pair, jnp.zeros((G, NB, FG), jnp.float32), (kernel, pair_list))
        irradiance = incoming / facet_areas[:, None, :]
        absorbed = jnp.sum(emissivity[:, :, None] * irradiance, axis=1)
        fourth = (absorbed + heat_load) / emit_sum
        radiosity = (weight_all * fourth[:, None, :] + (1.0 - emissivity[:, :, None]) * irradiance).astype(jnp.bfloat16)
    return radiosity, fourth ** 0.25
```

```python
import functools

import jax
import jax.numpy as jnp
from jax import lax
from jax.experimental import pallas as pl
from jax.experimental.pallas import tpu as pltpu
from jax.sharding import PartitionSpec as P

SWEEPS = 2
F32 = jnp.float32
BF16 = jnp.bfloat16


def exchange(kernel_dims, *refs):
    Z, X, C, S, ppd, NB, NM, NCLS = kernel_dims
    (
        pair_ref, coat_ref, emis_ref, share_ref,
        mat_hbm, start_hbm, areas_hbm, heat_hbm, kern_hbm, inc_ref,
        held, mats, kern, info, rows_out, rows_in, rad, gath, last,
        held_sem, mat_sem, kern_sem, info_send, info_recv, row_send, row_recv, send_sem, recv_sem,
    ) = refs
    z, x, c = lax.axis_index("grp"), lax.axis_index("band"), lax.axis_index("half")
    groups_dev, FG = mats.shape
    MESH = pl.DeviceIdType.MESH

    loads = [
        pltpu.make_async_copy(source, held.at[a], held_sem.at[a])
        for a, source in enumerate((start_hbm, areas_hbm, heat_hbm))
    ]
    loads.insert(0, pltpu.make_async_copy(mat_hbm, mats, mat_sem))
    for load in loads:
        load.start()
    load_kern = pltpu.make_async_copy(kern_hbm.at[pl.ds(x * ppd, ppd)], kern, kern_sem)
    load_kern.start()

    barrier = pltpu.get_barrier_semaphore()
    z_peers = [lax.rem(z + k, Z) for k in range(1, Z)]
    x_peers = [lax.rem(x + k, X) for k in range(1, X)]
    c_peers = [lax.rem(c + k, C) for k in range(1, C)]
    z_devices = [{"grp": t} for t in z_peers]
    c_devices = [{"half": t} for t in c_peers]
    far_devices = [{"grp": t, "half": u} for t in z_peers for u in c_peers]
    everyone = z_devices + c_devices + far_devices + [{"band": t} for t in x_peers]
    for peer in everyone:
        pl.semaphore_signal(barrier, inc=1, device_id=peer, device_id_type=MESH)

    width = X * S * NB
    per_tile = 128 // width
    mine_info = z * C + c
    lane = lax.broadcasted_iota(jnp.int32, (8, 128), 1)
    row = lax.broadcasted_iota(jnp.int32, (8, 128), 0)
    first_lane = lax.rem(mine_info, per_tile) * width
    slot_at = lane // NB - first_lane // NB
    keys = jnp.zeros((8, 128), jnp.int32)
    for xx in range(X):
        for s in range(S):
            group = pair_ref[xx * ppd + s % ppd, s // ppd]
            keys = jnp.where(slot_at == xx * S + s, group * NB + lane % NB, keys)
    columns = jnp.full((8, 128), -1, jnp.int32)
    band_of = lax.broadcasted_iota(jnp.int32, (S * NB, 128), 0)
    own_key = jnp.zeros((S * NB, 128), jnp.int32)
    for s in range(S):
        group = jnp.int32(0)
        for xx in range(X):
            group = jnp.where(x == xx, pair_ref[xx * ppd + s % ppd, s // ppd], group)
        columns = jnp.where(row == s, group, columns)
        own_key = jnp.where(band_of // NB == s, group * NB + band_of % NB, own_key)
    info[mine_info] = jnp.where(row == 7, keys, columns)

    pl.semaphore_wait(barrier, len(everyone))

    def info_copy(n, block, peer):
        return pltpu.make_async_remote_copy(
            src_ref=info.at[block],
            dst_ref=info.at[block],
            send_sem=info_send.at[n],
            recv_sem=info_recv.at[block],
            device_id=peer,
            device_id_type=MESH,
        )

    info_copies = []
    for n, peer in enumerate(z_devices + c_devices + far_devices):
        copy = info_copy(n, mine_info, peer)
        copy.start()
        info_copies.append(copy)
    coat = jnp.zeros((groups_dev, 1), jnp.int32)
    group_row = lax.broadcasted_iota(jnp.int32, (groups_dev, 1), 0)
    for g in range(groups_dev):
        coat = jnp.where(group_row == g, coat_ref[g], coat)
    for load in loads:
        load.wait()
    combined = (coat * NM + mats[...]).astype(F32)
    for t in z_peers:
        info_copy(0, t * C + c, everyone[0]).wait_recv()

    want = jnp.concatenate([info[t * C + c] for t in range(Z)], axis=0)[:, :groups_dev]
    local = lax.broadcasted_iota(jnp.int32, (Z * 8, groups_dev), 1) + z * groups_dev
    pick = jnp.where(want == local, jnp.ones(want.shape, F32), 0.0)
    row_copies = []
    for half in range(2):
        for a in range(2):
            source = combined if half + a == 0 else held[half * 2 + a - 1]
            found = jnp.dot(
                pick, source, precision=lax.Precision.HIGHEST, preferred_element_type=F32
            )
            for t in range(Z):
                rows_out[half, t, a * S : (a + 1) * S, :] = found[t * 8 : t * 8 + S, :]
        for k in range(1, Z):
            copy = pltpu.make_async_remote_copy(
                src_ref=rows_out.at[half, z_peers[k - 1]],
                dst_ref=rows_in.at[half, k - 1],
                send_sem=row_send.at[half, k - 1],
                recv_sem=row_recv.at[half, k - 1],
                device_id=z_devices[k - 1],
                device_id_type=MESH,
            )
            copy.start()
            row_copies.append(copy)

    def arrived(half):
        rows = rows_out[half, z]
        for k in range(1, Z):
            row_copies[half * (Z - 1) + k - 1].wait_recv()
            rows = rows + rows_in[half, k - 1]
        return rows

    band_col = lax.broadcasted_iota(jnp.int32, (NB, 1), 0)

    def table_column(ref, m):
        column = jnp.zeros((NB, 1), F32)
        for b in range(NB):
            column = jnp.where(band_col == b, ref[m, b], column)
        return column

    share_cols = [table_column(share_ref, m) for m in range(NM)]
    emis_cols = [table_column(emis_ref, k) for k in range(NCLS)]
    rows = arrived(0)
    weights, emis_slots, emit_sums = [], [], []
    for s in range(S):
        ids = rows[s : s + 1, :]
        emis = jnp.broadcast_to(emis_cols[0], (NB, FG))
        material = ids
        for k in range(1, NCLS):
            emis = jnp.where(ids > k * NM - 0.5, emis_cols[k], emis)
            material = jnp.where(ids > k * NM - 0.5, ids - k * NM, material)
        share = jnp.broadcast_to(share_cols[0], (NB, FG))
        for m in range(1, NM):
            share = jnp.where(material > m - 0.5, share_cols[m], share)
        weight = emis * share
        weights.append(weight)
        emis_slots.append(emis)
        emit_sums.append(jnp.sum(weight, axis=0, keepdims=True))
        rad[s] = (weight * rows[S + s : S + s + 1, :]).astype(BF16)
    load_kern.wait()

    def block_of(zz, xx, cc):
        return (zz * C + cc) * X + xx

    rows_block = S * NB
    for sweep in range(SWEEPS):
        mine = block_of(z, x, c)
        started = []
        final = sweep == SWEEPS - 1
        buffer = last if final else gath.at[sweep]

        def send(block, peer):
            copy = pltpu.make_async_remote_copy(
                src_ref=buffer.at[block],
                dst_ref=buffer.at[block],
                send_sem=send_sem.at[sweep, len(started)],
                recv_sem=recv_sem.at[sweep, block],
                device_id=peer,
                device_id_type=pl.DeviceIdType.MESH,
            )
            copy.start()
            started.append(copy)

        def receive(block):
            pltpu.make_async_remote_copy(
                src_ref=buffer.at[block],
                dst_ref=buffer.at[block],
                send_sem=send_sem.at[sweep, 0],
                recv_sem=recv_sem.at[sweep, block],
                device_id=everyone[0],
                device_id_type=pl.DeviceIdType.MESH,
            ).wait_recv()

        to_first, to_second = [], []
        for q in range(ppd):
            to_first.append(
                lax.dot_general(
                    rad[ppd + q], kern[q], (((1,), (1,)), ((), ())), preferred_element_type=F32
                )
            )
            to_second.append(jnp.dot(rad[q], kern[q], preferred_element_type=F32))
        buffer[mine] = jnp.concatenate(to_first + to_second, axis=0).astype(buffer.dtype)

        for t in z_peers:
            send(mine, {"grp": t})
        for t in x_peers:
            send(mine, {"band": t})
        for t in c_peers:
            send(mine, {"half": t})
        for xt in x_peers:
            block = block_of(z, xt, c)
            receive(block)
            for t in c_peers:
                send(block, {"half": t})
        for zt in z_peers:
            block = block_of(zt, x, c)
            receive(block)
            for t in x_peers:
                send(block, {"band": t})
            for t in c_peers:
                send(block, {"half": t})
        for zt in z_peers:
            for xt in x_peers:
                block = block_of(zt, xt, c)
                receive(block)
                for t in c_peers:
                    send(block, {"half": t})
        for ct in c_peers:
            for zt in [z] + z_peers:
                for xt in [x] + x_peers:
                    receive(block_of(zt, xt, ct))

        if sweep == 0:
            for t in z_peers + [z]:
                for u in c_peers:
                    info_copy(0, t * C + u, everyone[0]).wait_recv()
            tiles = []
            for t in range(Z * C // per_tile):
                tile = info[t * per_tile]
                for n in range(1, per_tile):
                    tile = tile + info[t * per_tile + n]
                tiles.append(tile[7:8, :])
            key_row = jnp.concatenate(tiles, axis=1)
            area_rows = arrived(1)

        terms = buffer[...].reshape(-1, FG)
        count = terms.shape[0]
        if not final:
            select = jnp.where(own_key[:, :1] == key_row, jnp.ones((rows_block, count), F32), 0.0)
            incoming = jnp.dot(select.astype(BF16), terms, preferred_element_type=F32)
            for s in range(S):
                emis = emis_slots[s]
                irradiance = incoming[s * NB : (s + 1) * NB, :] / area_rows[s : s + 1, :]
                absorbed = jnp.sum(emis * irradiance, axis=0, keepdims=True)
                fourth = (absorbed + area_rows[S + s : S + s + 1, :]) / emit_sums[s]
                rad[s] = (weights[s] * fourth + (1.0 - emis) * irradiance).astype(BF16)
        else:
            row_key = lax.broadcasted_iota(jnp.int32, (groups_dev * NB, count), 0) + z * (groups_dev * NB)
            select = jnp.where(row_key == key_row, jnp.ones(row_key.shape, F32), 0.0).astype(BF16)
            high = terms.astype(BF16)
            low = (terms - high.astype(F32)).astype(BF16)
            inc_ref[...] = jnp.dot(select, high, preferred_element_type=F32) + jnp.dot(
                select, low, preferred_element_type=F32
            )
        for copy in started:
            copy.wait_send()
    for copy in info_copies + row_copies:
        copy.wait_send()


def on_device(
    pair_list, kernel, facet_areas, heat_load, start_t4, material, coating, emis_table, share_table
):
    groups_dev, FG = facet_areas.shape
    NCLS, NB = emis_table.shape
    NM = share_table.shape[0]
    Z, X, C = lax.axis_size("grp"), lax.axis_size("band"), lax.axis_size("half")
    x = lax.axis_index("band")
    pairs_dev = pair_list.shape[0]
    ppd = pairs_dev // X
    S = 2 * ppd
    D = Z * X * C
    bands_dev = NB // X

    def emis_of(classes):
        result = jnp.zeros((classes.shape[0], NB), F32)
        for k in range(NCLS):
            result = jnp.where((classes == k)[:, None], emis_table[k][None, :], result)
        return result

    smem = pl.BlockSpec(memory_space=pltpu.SMEM)
    dma = pltpu.SemaphoreType.DMA
    incoming = pl.pallas_call(
        functools.partial(exchange, (Z, X, C, S, ppd, NB, NM, NCLS)),
        out_shape=jax.ShapeDtypeStruct((groups_dev * NB, FG), F32),
        in_specs=[smem] * 4 + [pl.BlockSpec(memory_space=pl.ANY)] * 5,
        out_specs=pl.BlockSpec(memory_space=pltpu.VMEM),
        scratch_shapes=[
            pltpu.VMEM((3, groups_dev, FG), F32),
            pltpu.VMEM((groups_dev, FG), jnp.int32),
            pltpu.VMEM((ppd, FG, FG), BF16),
            pltpu.VMEM((Z * C, 8, 128), jnp.int32),
            pltpu.VMEM((2, Z, 2 * S, FG), F32),
            pltpu.VMEM((2, Z - 1, 2 * S, FG), F32),
            pltpu.VMEM((S, NB, FG), BF16),
            pltpu.VMEM((SWEEPS - 1, D, S * NB, FG), BF16),
            pltpu.VMEM((D, S * NB, FG), F32),
            dma((3,)),
            dma(()),
            dma(()),
            dma((Z * C,)),
            dma((Z * C,)),
            dma((2, Z - 1)),
            dma((2, Z - 1)),
            dma((SWEEPS, D)),
            dma((SWEEPS, D)),
        ],
        compiler_params=pltpu.CompilerParams(
            collective_id=0, has_side_effects=True, vmem_limit_bytes=48 * 1024 * 1024
        ),
        cost_estimate=pl.CostEstimate(flops=200_000_000, bytes_accessed=8_000_000, transcendentals=0),
    )(
        pair_list, coating, emis_table, share_table,
        material, start_t4, facet_areas, heat_load, kernel,
    )

    emis = emis_of(coating)[:, :, None]
    share = jnp.zeros((groups_dev, NB, FG), F32)
    for m in range(NM):
        share = jnp.where((material == m)[:, None, :], share_table[m][None, :, None], share)
    weight = emis * share
    emit_sum = jnp.sum(weight, axis=1)
    irradiance = incoming.reshape(groups_dev, NB, FG) / facet_areas[:, None, :]
    absorbed = jnp.sum(emis * irradiance, axis=1)
    fourth = (absorbed + heat_load) / emit_sum

    def mine(rows):
        return lax.dynamic_slice_in_dim(rows, x * bands_dev, bands_dev, 1)

    share_mine = jnp.zeros((groups_dev, bands_dev, FG), F32)
    table = mine(share_table)
    for m in range(NM):
        share_mine = jnp.where((material == m)[:, None, :], table[m][None, :, None], share_mine)
    emis_mine = mine(emis)
    incoming_mine = mine(incoming.reshape(groups_dev, NB, FG))
    radiosity = emis_mine * share_mine * fourth[:, None, :] + (1.0 - emis_mine) * (
        incoming_mine / facet_areas[:, None, :]
    )
    return (radiosity.astype(BF16), fourth**0.25)


def solution(mesh):
    return jax.shard_map(
        on_device,
        mesh=mesh,
        in_specs=(
            P(("parts", "grp", "half"), None),
            P(("parts", "grp", "half"), None, None),
            P(("parts", "grp"), None),
            P(("parts", "grp"), None),
            P(("parts", "grp"), None),
            P(("parts", "grp"), None),
            P(("parts", "grp")),
            P(),
            P(),
        ),
        out_specs=(P(("parts", "grp"), "band", None), P(("parts", "grp"), None)),
        check_vma=False,
    )
```

```python
import functools

import jax
import jax.numpy as jnp
from jax import lax
from jax.experimental import pallas as pl
from jax.experimental.pallas import tpu as pltpu
from jax.sharding import PartitionSpec as P

SWEEPS = 2
F32 = jnp.float32
BF16 = jnp.bfloat16


def exchange(kernel_dims, *refs):
    Z, X, C, S, ppd, NB, NM, NCLS = kernel_dims
    slots, BD = X * S, NB // X
    (
        pair_ref, coat_ref, emis_ref, share_ref,
        mat_hbm, start_hbm, areas_hbm, heat_hbm, kern_hbm, inc_ref, absorbed_ref,
        held, mats, kern, info, rows_out, rows_in, rows_all, rad, stage, gath, last, sum_first, sum_last,
        held_sem, mat_sem, kern_sem, info_send, info_recv, row_send, row_recv,
        all_send, all_recv, sum_send, sum_recv, send_sem, recv_sem,
    ) = refs
    z, x, c = lax.axis_index("grp"), lax.axis_index("band"), lax.axis_index("half")
    groups_dev, FG = mats.shape
    MESH = pl.DeviceIdType.MESH

    loads = [
        pltpu.make_async_copy(source, held.at[a], held_sem.at[a])
        for a, source in enumerate((start_hbm, areas_hbm, heat_hbm))
    ]
    loads.insert(0, pltpu.make_async_copy(mat_hbm, mats, mat_sem))
    for load in loads:
        load.start()
    load_kern = pltpu.make_async_copy(kern_hbm, kern, kern_sem)
    load_kern.start()

    barrier = pltpu.get_barrier_semaphore()
    z_peers = [lax.rem(z + k, Z) for k in range(1, Z)]
    x_peers = [lax.rem(x + k, X) for k in range(1, X)]
    c_peers = [lax.rem(c + k, C) for k in range(1, C)]
    z_devices = [{"grp": t} for t in z_peers]
    x_devices = [{"band": t} for t in x_peers]
    c_devices = [{"half": t} for t in c_peers]
    far_devices = [{"grp": t, "half": u} for t in z_peers for u in c_peers]
    everyone = z_devices + c_devices + far_devices + x_devices
    for peer in everyone:
        pl.semaphore_signal(barrier, inc=1, device_id=peer, device_id_type=MESH)

    width = slots * BD
    per_tile = 128 // width
    mine_info = z * C + c
    lane = lax.broadcasted_iota(jnp.int32, (8, 128), 1)
    row = lax.broadcasted_iota(jnp.int32, (8, 128), 0)
    first_lane = lax.rem(mine_info, per_tile) * width
    slot_at = lane // BD - first_lane // BD
    keys = jnp.zeros((8, 128), jnp.int32)
    for xx in range(X):
        for s in range(S):
            group = pair_ref[xx * ppd + s % ppd, s // ppd]
            keys = jnp.where(slot_at == xx * S + s, group * BD + lane % BD, keys)
    columns = jnp.full((8, 128), -1, jnp.int32)
    band_of = lax.broadcasted_iota(jnp.int32, (slots * BD, 128), 0)
    own_key = jnp.zeros((slots * BD, 128), jnp.int32)
    for s in range(S):
        group = jnp.int32(0)
        for xx in range(X):
            here = pair_ref[xx * ppd + s % ppd, s // ppd]
            group = jnp.where(x == xx, here, group)
            own_key = jnp.where(band_of // BD == xx * S + s, here * BD + band_of % BD, own_key)
        columns = jnp.where(row == s, group, columns)
    info[mine_info] = jnp.where(row == 7, keys, columns)

    pl.semaphore_wait(barrier, len(everyone))

    def info_copy(n, block, peer):
        return pltpu.make_async_remote_copy(
            src_ref=info.at[block],
            dst_ref=info.at[block],
            send_sem=info_send.at[n],
            recv_sem=info_recv.at[block],
            device_id=peer,
            device_id_type=MESH,
        )

    info_copies = []
    for n, peer in enumerate(z_devices + c_devices + far_devices):
        copy = info_copy(n, mine_info, peer)
        copy.start()
        info_copies.append(copy)
    coat = jnp.zeros((groups_dev, 1), jnp.int32)
    group_row = lax.broadcasted_iota(jnp.int32, (groups_dev, 1), 0)
    for g in range(groups_dev):
        coat = jnp.where(group_row == g, coat_ref[g], coat)
    for load in loads:
        load.wait()
    combined = (coat * NM + mats[...]).astype(F32)
    for t in z_peers:
        info_copy(0, t * C + c, everyone[0]).wait_recv()

    want = jnp.concatenate([info[t * C + c] for t in range(Z)], axis=0)[:, :groups_dev]
    local = lax.broadcasted_iota(jnp.int32, (Z * 8, groups_dev), 1) + z * groups_dev
    pick = jnp.where(want == local, jnp.ones(want.shape, F32), 0.0)
    row_copies = []
    for half in range(2):
        for a in range(2):
            source = combined if half + a == 0 else held[half * 2 + a - 1]
            found = jnp.dot(
                pick, source, precision=lax.Precision.HIGHEST, preferred_element_type=F32
            )
            for t in range(Z):
                rows_out[half, t, a * S : (a + 1) * S, :] = found[t * 8 : t * 8 + S, :]
        for k in range(1, Z):
            copy = pltpu.make_async_remote_copy(
                src_ref=rows_out.at[half, z_peers[k - 1]],
                dst_ref=rows_in.at[half, k - 1],
                send_sem=row_send.at[half, k - 1],
                recv_sem=row_recv.at[half, k - 1],
                device_id=z_devices[k - 1],
                device_id_type=MESH,
            )
            copy.start()
            row_copies.append(copy)

    def over_band(buffer, send, recv):
        copies = [
            pltpu.make_async_remote_copy(
                src_ref=buffer.at[x],
                dst_ref=buffer.at[x],
                send_sem=send.at[n],
                recv_sem=recv.at[x],
                device_id=peer,
                device_id_type=MESH,
            )
            for n, peer in enumerate(x_devices)
        ]
        for copy in copies:
            copy.start()
        return copies

    def from_band(buffer, send, recv):
        for t in x_peers:
            pltpu.make_async_remote_copy(
                src_ref=buffer.at[t],
                dst_ref=buffer.at[t],
                send_sem=send.at[0],
                recv_sem=recv.at[t],
                device_id=everyone[0],
                device_id_type=MESH,
            ).wait_recv()

    band_copies = []

    def arrived(half):
        rows = rows_out[half, z]
        for k in range(1, Z):
            row_copies[half * (Z - 1) + k - 1].wait_recv()
            rows = rows + rows_in[half, k - 1]
        rows_all[half, x] = rows
        band_copies.extend(over_band(rows_all.at[half], all_send.at[half], all_recv.at[half]))

    band_col = lax.broadcasted_iota(jnp.int32, (BD, 1), 0)

    def own_column(ref, m):
        column = jnp.zeros((BD, 1), F32)
        for b in range(BD):
            value = ref[m, b]
            for xx in range(1, X):
                value = jnp.where(x == xx, ref[m, xx * BD + b], value)
            column = jnp.where(band_col == b, value, column)
        return column

    share_cols = [own_column(share_ref, m) for m in range(NM)]
    emis_cols = [own_column(emis_ref, k) for k in range(NCLS)]
    arrived(0)
    from_band(rows_all.at[0], all_send.at[0], all_recv.at[0])
    weights, emis_slots = [], []
    for n in range(slots):
        xx, s = n // S, n % S
        ids = rows_all[0, xx, s : s + 1, :]
        emis = jnp.broadcast_to(emis_cols[0], (BD, FG))
        material = ids
        for k in range(1, NCLS):
            emis = jnp.where(ids > k * NM - 0.5, emis_cols[k], emis)
            material = jnp.where(ids > k * NM - 0.5, ids - k * NM, material)
        share = jnp.broadcast_to(share_cols[0], (BD, FG))
        for m in range(1, NM):
            share = jnp.where(material > m - 0.5, share_cols[m], share)
        weight = emis * share
        weights.append(weight)
        emis_slots.append(emis)
        rad[n] = weight * rows_all[0, xx, S + s : S + s + 1, :]
    load_kern.wait()

    def block_of(zz, cc):
        return zz * C + cc

    rows_block = slots * BD
    for sweep in range(SWEEPS):
        mine = block_of(z, c)
        started = []
        final = sweep == SWEEPS - 1
        buffer = last if final else gath.at[sweep]

        def send(block, peer):
            copy = pltpu.make_async_remote_copy(
                src_ref=buffer.at[block],
                dst_ref=buffer.at[block],
                send_sem=send_sem.at[sweep, len(started)],
                recv_sem=recv_sem.at[sweep, block],
                device_id=peer,
                device_id_type=pl.DeviceIdType.MESH,
            )
            copy.start()
            started.append(copy)

        def receive(block):
            pltpu.make_async_remote_copy(
                src_ref=buffer.at[block],
                dst_ref=buffer.at[block],
                send_sem=send_sem.at[sweep, 0],
                recv_sem=recv_sem.at[sweep, block],
                device_id=everyone[0],
                device_id_type=pl.DeviceIdType.MESH,
            ).wait_recv()

        for n in range(slots):
            xx, end, q = n // S, n % S // ppd, n % ppd
            pair = kern[xx * ppd + q]
            if end == 0:
                term = lax.dot_general(
                    rad[n + ppd].astype(BF16), pair, (((1,), (1,)), ((), ())), preferred_element_type=F32
                )
            else:
                term = jnp.dot(rad[n - ppd].astype(BF16), pair, preferred_element_type=F32)
            stage[n * BD : (n + 1) * BD, :] = term
        buffer[mine] = stage[...].astype(buffer.dtype)

        for peer in z_devices + c_devices:
            send(mine, peer)
        if not final:
            arrived(1)
            emit_sums = []
            for n in range(slots):
                ids = rows_all[0, n // S, n % S : n % S + 1, :]
                emit_sum = jnp.zeros((1, FG), F32)
                for k in range(NCLS):
                    for m in range(NM):
                        total = emis_ref[k, 0] * share_ref[m, 0]
                        for b in range(1, NB):
                            total = total + emis_ref[k, b] * share_ref[m, b]
                        emit_sum = jnp.where(ids > k * NM + m - 0.5, total, emit_sum)
                emit_sums.append(emit_sum)
            from_band(rows_all.at[1], all_send.at[1], all_recv.at[1])
        for zt in z_peers:
            receive(block_of(zt, c))
            for peer in c_devices:
                send(block_of(zt, c), peer)
        for ct in c_peers:
            for zt in [z] + z_peers:
                receive(block_of(zt, ct))

        if sweep == 0:
            for t in z_peers + [z]:
                for u in c_peers:
                    info_copy(0, t * C + u, everyone[0]).wait_recv()
            tiles = []
            for t in range(Z * C // per_tile):
                tile = info[t * per_tile]
                for n in range(1, per_tile):
                    tile = tile + info[t * per_tile + n]
                tiles.append(tile[7:8, :])
            key_row = jnp.concatenate(tiles, axis=1)

        terms = buffer[...].reshape(-1, FG)
        count = terms.shape[0]
        if not final:
            select = jnp.where(own_key[:, :1] == key_row, jnp.ones((rows_block, count), F32), 0.0)
            incoming = jnp.dot(select.astype(BF16), terms, preferred_element_type=F32)
            stage[...] = incoming
            for n in range(slots):
                xx, s = n // S, n % S
                irradiance = stage[n * BD : (n + 1) * BD, :] / rows_all[1, xx, s : s + 1, :]
                stage[n * BD : (n + 1) * BD, :] = irradiance
                sum_first[x, n : n + 1, :] = jnp.sum(emis_slots[n] * irradiance, axis=0, keepdims=True)
            band_copies.extend(over_band(sum_first, sum_send.at[0], sum_recv.at[0]))
            from_band(sum_first, sum_send.at[0], sum_recv.at[0])
            absorbed = sum_first[0]
            for xx in range(1, X):
                absorbed = absorbed + sum_first[xx]
            for n in range(slots):
                xx, s = n // S, n % S
                fourth = (absorbed[n : n + 1, :] + rows_all[1, xx, S + s : S + s + 1, :]) / emit_sums[n]
                irradiance = stage[n * BD : (n + 1) * BD, :]
                rad[n] = weights[n] * fourth + (1.0 - emis_slots[n]) * irradiance
        else:
            row_key = lax.broadcasted_iota(jnp.int32, (groups_dev * BD, count), 0) + z * (groups_dev * BD)
            select = jnp.where(row_key == key_row, jnp.ones(row_key.shape, F32), 0.0).astype(BF16)
            high = terms.astype(BF16)
            low = (terms - high.astype(F32)).astype(BF16)
            inc_ref[...] = jnp.dot(select, high, preferred_element_type=F32) + jnp.dot(
                select, low, preferred_element_type=F32
            )
            for g in range(groups_dev):
                emis = emis_cols[0]
                for k in range(1, NCLS):
                    emis = jnp.where(coat_ref[g] == k, emis_cols[k], emis)
                received = emis * inc_ref[g * BD : (g + 1) * BD, :]
                sum_last[x, g : g + 1, :] = jnp.sum(received, axis=0, keepdims=True) / held[1, g : g + 1, :]
            band_copies.extend(over_band(sum_last, sum_send.at[1], sum_recv.at[1]))
            from_band(sum_last, sum_send.at[1], sum_recv.at[1])
            absorbed = sum_last[0]
            for xx in range(1, X):
                absorbed = absorbed + sum_last[xx]
            absorbed_ref[...] = absorbed
        for copy in started:
            copy.wait_send()
    for copy in info_copies + row_copies + band_copies:
        copy.wait_send()


def on_device(
    pair_list, kernel, facet_areas, heat_load, start_t4, material, coating, emis_table, share_table
):
    groups_dev, FG = facet_areas.shape
    NCLS, NB = emis_table.shape
    NM = share_table.shape[0]
    Z, X, C = lax.axis_size("grp"), lax.axis_size("band"), lax.axis_size("half")
    x = lax.axis_index("band")
    pairs_dev = pair_list.shape[0]
    ppd = pairs_dev // X
    S = 2 * ppd
    D = Z * C
    bands_dev = NB // X

    def emis_of(classes):
        result = jnp.zeros((classes.shape[0], NB), F32)
        for k in range(NCLS):
            result = jnp.where((classes == k)[:, None], emis_table[k][None, :], result)
        return result

    smem = pl.BlockSpec(memory_space=pltpu.SMEM)
    dma = pltpu.SemaphoreType.DMA
    incoming, absorbed = pl.pallas_call(
        functools.partial(exchange, (Z, X, C, S, ppd, NB, NM, NCLS)),
        out_shape=(
            jax.ShapeDtypeStruct((groups_dev * bands_dev, FG), F32),
            jax.ShapeDtypeStruct((groups_dev, FG), F32),
        ),
        in_specs=[smem] * 4 + [pl.BlockSpec(memory_space=pl.ANY)] * 5,
        out_specs=(pl.BlockSpec(memory_space=pltpu.VMEM),) * 2,
        scratch_shapes=[
            pltpu.VMEM((3, groups_dev, FG), F32),
            pltpu.VMEM((groups_dev, FG), jnp.int32),
            pltpu.VMEM((pairs_dev, FG, FG), BF16),
            pltpu.VMEM((Z * C, 8, 128), jnp.int32),
            pltpu.VMEM((2, Z, 2 * S, FG), F32),
            pltpu.VMEM((2, Z - 1, 2 * S, FG), F32),
            pltpu.VMEM((2, X, 2 * S, FG), F32),
            pltpu.VMEM((2 * pairs_dev, bands_dev, FG), F32),
            pltpu.VMEM((2 * pairs_dev * bands_dev, FG), F32),
            pltpu.VMEM((SWEEPS - 1, D, 2 * pairs_dev * bands_dev, FG), BF16),
            pltpu.VMEM((D, 2 * pairs_dev * bands_dev, FG), F32),
            pltpu.VMEM((X, 2 * pairs_dev, FG), F32),
            pltpu.VMEM((X, groups_dev, FG), F32),
            dma((3,)),
            dma(()),
            dma(()),
            dma((Z * C,)),
            dma((Z * C,)),
            dma((2, Z - 1)),
            dma((2, Z - 1)),
            dma((2, X - 1)),
            dma((2, X)),
            dma((2, X - 1)),
            dma((2, X)),
            dma((SWEEPS, 2 * D)),
            dma((SWEEPS, D)),
        ],
        compiler_params=pltpu.CompilerParams(
            collective_id=0, has_side_effects=True, vmem_limit_bytes=60 * 1024 * 1024
        ),
        cost_estimate=pl.CostEstimate(flops=200_000_000, bytes_accessed=8_000_000, transcendentals=0),
    )(
        pair_list, coating, emis_table, share_table,
        material, start_t4, facet_areas, heat_load, kernel,
    )

    emis = emis_of(coating)[:, :, None]
    share = jnp.zeros((groups_dev, NB, FG), F32)
    for m in range(NM):
        share = jnp.where((material == m)[:, None, :], share_table[m][None, :, None], share)
    weight = emis * share
    emit_sum = jnp.sum(weight, axis=1)
    fourth = (absorbed + heat_load) / emit_sum

    def mine(rows):
        return lax.dynamic_slice_in_dim(rows, x * bands_dev, bands_dev, 1)

    share_mine = jnp.zeros((groups_dev, bands_dev, FG), F32)
    table = mine(share_table)
    for m in range(NM):
        share_mine = jnp.where((material == m)[:, None, :], table[m][None, :, None], share_mine)
    emis_mine = mine(emis)
    incoming_mine = incoming.reshape(groups_dev, bands_dev, FG)
    radiosity = emis_mine * share_mine * fourth[:, None, :] + (1.0 - emis_mine) * (
        incoming_mine / facet_areas[:, None, :]
    )
    return (radiosity.astype(BF16), fourth**0.25)


def solution(mesh):
    return jax.shard_map(
        on_device,
        mesh=mesh,
        in_specs=(
            P(("parts", "grp", "half"), None),
            P(("parts", "grp", "half"), None, None),
            P(("parts", "grp"), None),
            P(("parts", "grp"), None),
            P(("parts", "grp"), None),
            P(("parts", "grp"), None),
            P(("parts", "grp")),
            P(),
            P(),
        ),
        out_specs=(P(("parts", "grp"), "band", None), P(("parts", "grp"), None)),
        check_vma=False,
    )
```

```python
import functools

import jax
import jax.numpy as jnp
from jax import lax
from jax.experimental import pallas as pl
from jax.experimental.pallas import tpu as pltpu
from jax.sharding import PartitionSpec as P

SWEEPS = 2
F32 = jnp.float32
BF16 = jnp.bfloat16


def exchange(kernel_dims, *refs):
    Z, X, C, S, ppd, NB, NM, NCLS = kernel_dims
    slots, BD = X * S, NB // X
    (
        pair_ref, coat_ref, emis_ref, share_ref,
        mat_hbm, start_hbm, areas_hbm, heat_hbm, kern_hbm, inc_ref, fourth_ref,
        held, mats, ident, kern, info, rows_out, rows_in, rows_all, rad, stage, gath, last, sum_first, sum_last, emit_held, inc_all,
        held_sem, mat_sem, kern_sem, info_send, info_recv, row_send, row_recv,
        all_send, all_recv, sum_send, sum_recv, send_sem, recv_sem,
    ) = refs
    z, x, c = lax.axis_index("grp"), lax.axis_index("band"), lax.axis_index("half")
    groups_dev, FG = mats.shape
    MESH = pl.DeviceIdType.MESH

    loads = [
        pltpu.make_async_copy(source, held.at[a], held_sem.at[a])
        for a, source in enumerate((start_hbm, areas_hbm, heat_hbm))
    ]
    loads.insert(0, pltpu.make_async_copy(mat_hbm, mats, mat_sem))
    for load in loads:
        load.start()
    load_kern = pltpu.make_async_copy(kern_hbm, kern, kern_sem)
    load_kern.start()

    barrier = pltpu.get_barrier_semaphore()
    z_peers = [lax.rem(z + k, Z) for k in range(1, Z)]
    x_peers = [lax.rem(x + k, X) for k in range(1, X)]
    c_peers = [lax.rem(c + k, C) for k in range(1, C)]
    z_devices = [{"grp": t} for t in z_peers]
    x_devices = [{"band": t} for t in x_peers]
    c_devices = [{"half": t} for t in c_peers]
    far_devices = [{"grp": t, "half": u} for t in z_peers for u in c_peers]
    everyone = z_devices + c_devices + far_devices + x_devices
    for peer in everyone:
        pl.semaphore_signal(barrier, inc=1, device_id=peer, device_id_type=MESH)

    width = slots * BD
    per_tile = 128 // width
    mine_info = z * C + c
    lane = lax.broadcasted_iota(jnp.int32, (8, 128), 1)
    row = lax.broadcasted_iota(jnp.int32, (8, 128), 0)
    first_lane = lax.rem(mine_info, per_tile) * width
    slot_at = lane // BD - first_lane // BD
    keys = jnp.zeros((8, 128), jnp.int32)
    for xx in range(X):
        for s in range(S):
            group = pair_ref[xx * ppd + s % ppd, s // ppd]
            keys = jnp.where(slot_at == xx * S + s, group * BD + lane % BD, keys)
    columns = jnp.full((8, 128), -1, jnp.int32)
    band_of = lax.broadcasted_iota(jnp.int32, (slots * BD, 128), 0)
    own_key = jnp.zeros((slots * BD, 128), jnp.int32)
    for s in range(S):
        group = jnp.int32(0)
        for xx in range(X):
            here = pair_ref[xx * ppd + s % ppd, s // ppd]
            group = jnp.where(x == xx, here, group)
            own_key = jnp.where(band_of // BD == xx * S + s, here * BD + band_of % BD, own_key)
        columns = jnp.where(row == s, group, columns)
    info[mine_info] = jnp.where(row == 7, keys, columns)

    pl.semaphore_wait(barrier, len(everyone))

    def info_copy(n, block, peer):
        return pltpu.make_async_remote_copy(
            src_ref=info.at[block],
            dst_ref=info.at[block],
            send_sem=info_send.at[n],
            recv_sem=info_recv.at[block],
            device_id=peer,
            device_id_type=MESH,
        )

    info_copies = []
    for n, peer in enumerate(z_devices + c_devices + far_devices):
        copy = info_copy(n, mine_info, peer)
        copy.start()
        info_copies.append(copy)
    coat = jnp.zeros((groups_dev, 1), jnp.int32)
    group_row = lax.broadcasted_iota(jnp.int32, (groups_dev, 1), 0)
    for g in range(groups_dev):
        coat = jnp.where(group_row == g, coat_ref[g], coat)
    for load in loads:
        load.wait()
    ident[...] = (coat * NM + mats[...]).astype(F32)
    for t in z_peers:
        info_copy(0, t * C + c, everyone[0]).wait_recv()

    want = jnp.concatenate([info[t * C + c] for t in range(Z)], axis=0)[:, :groups_dev]
    local = lax.broadcasted_iota(jnp.int32, (Z * 8, groups_dev), 1) + z * groups_dev
    pick = jnp.where(want == local, jnp.ones(want.shape, F32), 0.0)
    pick3 = jnp.concatenate([pick] * 3, axis=1).astype(BF16)
    pick = pick.astype(BF16)
    row_copies = []
    for half in range(2):
        for a in range(2):
            if half + a == 0:
                found = jnp.dot(pick, ident[...].astype(BF16), preferred_element_type=F32)
            else:
                source = held[half * 2 + a - 1]
                high = source.astype(BF16)
                rest = source - high.astype(F32)
                middle = rest.astype(BF16)
                low = (rest - middle.astype(F32)).astype(BF16)
                parts = jnp.concatenate([high, middle, low], axis=0)
                found = jnp.dot(pick3, parts, preferred_element_type=F32)
            for t in range(Z):
                rows_out[half, t, a * S : (a + 1) * S, :] = found[t * 8 : t * 8 + S, :]
        for k in range(1, Z):
            copy = pltpu.make_async_remote_copy(
                src_ref=rows_out.at[half, z_peers[k - 1]],
                dst_ref=rows_in.at[half, k - 1],
                send_sem=row_send.at[half, k - 1],
                recv_sem=row_recv.at[half, k - 1],
                device_id=z_devices[k - 1],
                device_id_type=MESH,
            )
            copy.start()
            row_copies.append(copy)

    def over_band(buffer, send, recv):
        copies = [
            pltpu.make_async_remote_copy(
                src_ref=buffer.at[x],
                dst_ref=buffer.at[x],
                send_sem=send.at[n],
                recv_sem=recv.at[x],
                device_id=peer,
                device_id_type=MESH,
            )
            for n, peer in enumerate(x_devices)
        ]
        for copy in copies:
            copy.start()
        return copies

    def from_band(buffer, send, recv):
        for t in x_peers:
            pltpu.make_async_remote_copy(
                src_ref=buffer.at[t],
                dst_ref=buffer.at[t],
                send_sem=send.at[0],
                recv_sem=recv.at[t],
                device_id=everyone[0],
                device_id_type=MESH,
            ).wait_recv()

    band_copies = []

    def arrived(half):
        rows = rows_out[half, z]
        for k in range(1, Z):
            row_copies[half * (Z - 1) + k - 1].wait_recv()
            rows = rows + rows_in[half, k - 1]
        rows_all[half, x] = rows
        band_copies.extend(over_band(rows_all.at[half], all_send.at[half], all_recv.at[half]))

    band_col = lax.broadcasted_iota(jnp.int32, (BD, 1), 0)

    def own_column(ref, m):
        column = jnp.zeros((BD, 1), F32)
        for b in range(BD):
            value = ref[m, b]
            for xx in range(1, X):
                value = jnp.where(x == xx, ref[m, xx * BD + b], value)
            column = jnp.where(band_col == b, value, column)
        return column

    share_cols = [own_column(share_ref, m) for m in range(NM)]
    emis_cols = [own_column(emis_ref, k) for k in range(NCLS)]
    arrived(0)
    from_band(rows_all.at[0], all_send.at[0], all_recv.at[0])
    weights, emis_slots = [], []
    for n in range(slots):
        xx, s = n // S, n % S
        ids = rows_all[0, xx, s : s + 1, :]
        emis = jnp.broadcast_to(emis_cols[0], (BD, FG))
        material = ids
        for k in range(1, NCLS):
            emis = jnp.where(ids > k * NM - 0.5, emis_cols[k], emis)
            material = jnp.where(ids > k * NM - 0.5, ids - k * NM, material)
        share = jnp.broadcast_to(share_cols[0], (BD, FG))
        for m in range(1, NM):
            share = jnp.where(material > m - 0.5, share_cols[m], share)
        weight = emis * share
        weights.append(weight)
        emis_slots.append(emis)
        rad[n] = weight * rows_all[0, xx, S + s : S + s + 1, :]
    load_kern.wait()

    def block_of(zz, cc):
        return zz * C + cc

    totals = []
    for k in range(NCLS):
        for m in range(NM):
            total = emis_ref[k, 0] * share_ref[m, 0]
            for b in range(1, NB):
                total = total + emis_ref[k, b] * share_ref[m, b]
            totals.append(total)

    def emit_of(ids):
        emit_sum = jnp.full(ids.shape, totals[0], F32)
        for n in range(1, len(totals)):
            emit_sum = jnp.where(ids > n - 0.5, totals[n], emit_sum)
        return emit_sum

    rows_block = slots * BD
    for sweep in range(SWEEPS):
        mine = block_of(z, c)
        started = []
        final = sweep == SWEEPS - 1
        buffer = last if final else gath.at[sweep]

        def send(block, peer):
            copy = pltpu.make_async_remote_copy(
                src_ref=buffer.at[block],
                dst_ref=buffer.at[block],
                send_sem=send_sem.at[sweep, len(started)],
                recv_sem=recv_sem.at[sweep, block],
                device_id=peer,
                device_id_type=pl.DeviceIdType.MESH,
            )
            copy.start()
            started.append(copy)

        def receive(block):
            pltpu.make_async_remote_copy(
                src_ref=buffer.at[block],
                dst_ref=buffer.at[block],
                send_sem=send_sem.at[sweep, 0],
                recv_sem=recv_sem.at[sweep, block],
                device_id=everyone[0],
                device_id_type=pl.DeviceIdType.MESH,
            ).wait_recv()

        for n in range(slots):
            xx, end, q = n // S, n % S // ppd, n % ppd
            pair = kern[xx * ppd + q]
            if end == 0:
                term = lax.dot_general(
                    rad[n + ppd].astype(BF16), pair, (((1,), (1,)), ((), ())), preferred_element_type=F32
                )
            else:
                term = jnp.dot(rad[n - ppd].astype(BF16), pair, preferred_element_type=F32)
            stage[n * BD : (n + 1) * BD, :] = term
        buffer[mine] = stage[...].astype(buffer.dtype)

        for peer in z_devices + c_devices:
            send(mine, peer)
        if not final:
            arrived(1)
            emit_rows = [emit_of(rows_all[0, xx, :S, :]) for xx in range(X)]
            emit_sums = [emit_rows[n // S][n % S : n % S + 1, :] for n in range(slots)]
            from_band(rows_all.at[1], all_send.at[1], all_recv.at[1])
        else:
            emit_held[...] = emit_of(ident[...])
        for zt in z_peers:
            receive(block_of(zt, c))
            for peer in c_devices:
                send(block_of(zt, c), peer)
        for ct in c_peers:
            for zt in [z] + z_peers:
                receive(block_of(zt, ct))

        if sweep == 0:
            for t in z_peers + [z]:
                for u in c_peers:
                    info_copy(0, t * C + u, everyone[0]).wait_recv()
            tiles = []
            for t in range(Z * C // per_tile):
                tile = info[t * per_tile]
                for n in range(1, per_tile):
                    tile = tile + info[t * per_tile + n]
                tiles.append(tile[7:8, :])
            key_row = jnp.concatenate(tiles, axis=1)

        terms = buffer[...].reshape(-1, FG)
        count = terms.shape[0]
        if not final:
            select = jnp.where(own_key[:, :1] == key_row, jnp.ones((rows_block, count), F32), 0.0)
            incoming = jnp.dot(select.astype(BF16), terms, preferred_element_type=F32)
            stage[...] = incoming
            for n in range(slots):
                xx, s = n // S, n % S
                irradiance = stage[n * BD : (n + 1) * BD, :] / rows_all[1, xx, s : s + 1, :]
                stage[n * BD : (n + 1) * BD, :] = irradiance
                sum_first[x, n : n + 1, :] = jnp.sum(emis_slots[n] * irradiance, axis=0, keepdims=True)
            band_copies.extend(over_band(sum_first, sum_send.at[0], sum_recv.at[0]))
            from_band(sum_first, sum_send.at[0], sum_recv.at[0])
            absorbed = sum_first[0]
            for xx in range(1, X):
                absorbed = absorbed + sum_first[xx]
            for n in range(slots):
                xx, s = n // S, n % S
                fourth = (absorbed[n : n + 1, :] + rows_all[1, xx, S + s : S + s + 1, :]) / emit_sums[n]
                irradiance = stage[n * BD : (n + 1) * BD, :]
                rad[n] = weights[n] * fourth + (1.0 - emis_slots[n]) * irradiance
        else:
            row_key = lax.broadcasted_iota(jnp.int32, (groups_dev * BD, count), 0) + z * (groups_dev * BD)
            select = jnp.where(row_key == key_row, jnp.ones(row_key.shape, F32), 0.0).astype(BF16)
            high = terms.astype(BF16)
            low = (terms - high.astype(F32)).astype(BF16)
            inc_all[...] = jnp.dot(select, high, preferred_element_type=F32) + jnp.dot(
                select, low, preferred_element_type=F32
            )
            for g in range(groups_dev):
                emis = emis_cols[0]
                for k in range(1, NCLS):
                    emis = jnp.where(coat_ref[g] == k, emis_cols[k], emis)
                piece = inc_all[g * BD : (g + 1) * BD, :]
                received = emis * piece
                inc_ref[g] = piece
                sum_last[x, g : g + 1, :] = jnp.sum(received, axis=0, keepdims=True) / held[1, g : g + 1, :]
            band_copies.extend(over_band(sum_last, sum_send.at[1], sum_recv.at[1]))
            from_band(sum_last, sum_send.at[1], sum_recv.at[1])
            absorbed = sum_last[0]
            for xx in range(1, X):
                absorbed = absorbed + sum_last[xx]
            fourth_ref[...] = (absorbed + held[2]) / emit_held[...]
        for copy in started:
            copy.wait_send()
    for copy in info_copies + row_copies + band_copies:
        copy.wait_send()


def on_device(
    pair_list, kernel, facet_areas, heat_load, start_t4, material, coating, emis_table, share_table
):
    groups_dev, FG = facet_areas.shape
    NCLS, NB = emis_table.shape
    NM = share_table.shape[0]
    Z, X, C = lax.axis_size("grp"), lax.axis_size("band"), lax.axis_size("half")
    x = lax.axis_index("band")
    pairs_dev = pair_list.shape[0]
    ppd = pairs_dev // X
    S = 2 * ppd
    D = Z * C
    bands_dev = NB // X

    def emis_of(classes):
        result = jnp.zeros((classes.shape[0], NB), F32)
        for k in range(NCLS):
            result = jnp.where((classes == k)[:, None], emis_table[k][None, :], result)
        return result

    smem = pl.BlockSpec(memory_space=pltpu.SMEM)
    dma = pltpu.SemaphoreType.DMA
    incoming, fourth = pl.pallas_call(
        functools.partial(exchange, (Z, X, C, S, ppd, NB, NM, NCLS)),
        out_shape=(
            jax.ShapeDtypeStruct((groups_dev, bands_dev, FG), F32),
            jax.ShapeDtypeStruct((groups_dev, FG), F32),
        ),
        in_specs=[smem] * 4 + [pl.BlockSpec(memory_space=pl.ANY)] * 5,
        out_specs=(pl.BlockSpec(memory_space=pltpu.VMEM),) * 2,
        scratch_shapes=[
            pltpu.VMEM((3, groups_dev, FG), F32),
            pltpu.VMEM((groups_dev, FG), jnp.int32),
            pltpu.VMEM((groups_dev, FG), F32),
            pltpu.VMEM((pairs_dev, FG, FG), BF16),
            pltpu.VMEM((Z * C, 8, 128), jnp.int32),
            pltpu.VMEM((2, Z, 2 * S, FG), F32),
            pltpu.VMEM((2, Z - 1, 2 * S, FG), F32),
            pltpu.VMEM((2, X, 2 * S, FG), F32),
            pltpu.VMEM((2 * pairs_dev, bands_dev, FG), F32),
            pltpu.VMEM((2 * pairs_dev * bands_dev, FG), F32),
            pltpu.VMEM((SWEEPS - 1, D, 2 * pairs_dev * bands_dev, FG), BF16),
            pltpu.VMEM((D, 2 * pairs_dev * bands_dev, FG), F32),
            pltpu.VMEM((X, 2 * pairs_dev, FG), F32),
            pltpu.VMEM((X, groups_dev, FG), F32),
            pltpu.VMEM((groups_dev, FG), F32),
            pltpu.VMEM((groups_dev * bands_dev, FG), F32),
            dma((3,)),
            dma(()),
            dma(()),
            dma((Z * C,)),
            dma((Z * C,)),
            dma((2, Z - 1)),
            dma((2, Z - 1)),
            dma((2, X - 1)),
            dma((2, X)),
            dma((2, X - 1)),
            dma((2, X)),
            dma((SWEEPS, 2 * D)),
            dma((SWEEPS, D)),
        ],
        compiler_params=pltpu.CompilerParams(
            collective_id=0, has_side_effects=True, vmem_limit_bytes=60 * 1024 * 1024
        ),
        cost_estimate=pl.CostEstimate(flops=200_000_000, bytes_accessed=8_000_000, transcendentals=0),
    )(
        pair_list, coating, emis_table, share_table,
        material, start_t4, facet_areas, heat_load, kernel,
    )

    emis = emis_of(coating)[:, :, None]

    def mine(rows):
        return lax.dynamic_slice_in_dim(rows, x * bands_dev, bands_dev, 1)

    share_mine = jnp.zeros((groups_dev, bands_dev, FG), F32)
    table = mine(share_table)
    for m in range(NM):
        share_mine = jnp.where((material == m)[:, None, :], table[m][None, :, None], share_mine)
    emis_mine = mine(emis)
    radiosity = emis_mine * share_mine * fourth[:, None, :] + (1.0 - emis_mine) * (
        incoming / facet_areas[:, None, :]
    )
    return (radiosity.astype(BF16), fourth**0.25)


def solution(mesh):
    return jax.shard_map(
        on_device,
        mesh=mesh,
        in_specs=(
            P(("parts", "grp", "half"), None),
            P(("parts", "grp", "half"), None, None),
            P(("parts", "grp"), None),
            P(("parts", "grp"), None),
            P(("parts", "grp"), None),
            P(("parts", "grp"), None),
            P(("parts", "grp")),
            P(),
            P(),
        ),
        out_specs=(P(("parts", "grp"), "band", None), P(("parts", "grp"), None)),
        check_vma=False,
    )
```

```python
import functools

import jax
import jax.numpy as jnp
from jax import lax
from jax.experimental import pallas as pl
from jax.experimental.pallas import tpu as pltpu
from jax.sharding import PartitionSpec as P

SWEEPS = 2
F32 = jnp.float32
BF16 = jnp.bfloat16


def exchange(kernel_dims, *refs):
    Z, X, C, S, ppd, NB, NM, NCLS = kernel_dims
    slots, BD = X * S, NB // X
    (
        pair_ref, coat_ref, emis_ref, share_ref,
        mat_hbm, start_hbm, areas_hbm, heat_hbm, kern_hbm, out_ref, fourth_ref,
        held, mats, ident, kern, info, rows_out, rows_in, rows_all, rad, stage, gath, last, sum_first, sum_last, emit_held, inc_all, weight_held,
        held_sem, mat_sem, kern_sem, info_send, info_recv, row_send, row_recv,
        all_send, all_recv, sum_send, sum_recv, send_sem, recv_sem,
    ) = refs
    z, x, c = lax.axis_index("grp"), lax.axis_index("band"), lax.axis_index("half")
    groups_dev, FG = mats.shape
    MESH = pl.DeviceIdType.MESH

    loads = [
        pltpu.make_async_copy(source, held.at[a], held_sem.at[a])
        for a, source in enumerate((start_hbm, areas_hbm, heat_hbm))
    ]
    loads.insert(0, pltpu.make_async_copy(mat_hbm, mats, mat_sem))
    for load in loads:
        load.start()
    load_kern = pltpu.make_async_copy(kern_hbm, kern, kern_sem)
    load_kern.start()

    barrier = pltpu.get_barrier_semaphore()
    z_peers = [lax.rem(z + k, Z) for k in range(1, Z)]
    x_peers = [lax.rem(x + k, X) for k in range(1, X)]
    c_peers = [lax.rem(c + k, C) for k in range(1, C)]
    z_devices = [{"grp": t} for t in z_peers]
    x_devices = [{"band": t} for t in x_peers]
    c_devices = [{"half": t} for t in c_peers]
    far_devices = [{"grp": t, "half": u} for t in z_peers for u in c_peers]
    everyone = z_devices + c_devices + far_devices + x_devices
    for peer in everyone:
        pl.semaphore_signal(barrier, inc=1, device_id=peer, device_id_type=MESH)

    width = slots * BD
    per_tile = 128 // width
    mine_info = z * C + c
    lane = lax.broadcasted_iota(jnp.int32, (8, 128), 1)
    row = lax.broadcasted_iota(jnp.int32, (8, 128), 0)
    first_lane = lax.rem(mine_info, per_tile) * width
    slot_at = lane // BD - first_lane // BD
    keys = jnp.zeros((8, 128), jnp.int32)
    for xx in range(X):
        for s in range(S):
            group = pair_ref[xx * ppd + s % ppd, s // ppd]
            keys = jnp.where(slot_at == xx * S + s, group * BD + lane % BD, keys)
    columns = jnp.full((8, 128), -1, jnp.int32)
    band_of = lax.broadcasted_iota(jnp.int32, (slots * BD, 128), 0)
    own_key = jnp.zeros((slots * BD, 128), jnp.int32)
    for s in range(S):
        group = jnp.int32(0)
        for xx in range(X):
            here = pair_ref[xx * ppd + s % ppd, s // ppd]
            group = jnp.where(x == xx, here, group)
            own_key = jnp.where(band_of // BD == xx * S + s, here * BD + band_of % BD, own_key)
        columns = jnp.where(row == s, group, columns)
    info[mine_info] = jnp.where(row == 7, keys, columns)

    pl.semaphore_wait(barrier, len(everyone))

    def info_copy(n, block, peer):
        return pltpu.make_async_remote_copy(
            src_ref=info.at[block],
            dst_ref=info.at[block],
            send_sem=info_send.at[n],
            recv_sem=info_recv.at[block],
            device_id=peer,
            device_id_type=MESH,
        )

    info_copies = []
    for n, peer in enumerate(z_devices + c_devices + far_devices):
        copy = info_copy(n, mine_info, peer)
        copy.start()
        info_copies.append(copy)
    coat = jnp.zeros((groups_dev, 1), jnp.int32)
    group_row = lax.broadcasted_iota(jnp.int32, (groups_dev, 1), 0)
    for g in range(groups_dev):
        coat = jnp.where(group_row == g, coat_ref[g], coat)
    for load in loads:
        load.wait()
    ident[...] = (coat * NM + mats[...]).astype(F32)
    for t in z_peers:
        info_copy(0, t * C + c, everyone[0]).wait_recv()

    want = jnp.concatenate([info[t * C + c] for t in range(Z)], axis=0)[:, :groups_dev]
    local = lax.broadcasted_iota(jnp.int32, (Z * 8, groups_dev), 1) + z * groups_dev
    pick = jnp.where(want == local, jnp.ones(want.shape, F32), 0.0)
    pick3 = jnp.concatenate([pick] * 3, axis=1).astype(BF16)
    pick = pick.astype(BF16)
    row_copies = []
    for half in range(2):
        for a in range(2):
            if half + a == 0:
                found = jnp.dot(pick, ident[...].astype(BF16), preferred_element_type=F32)
            else:
                source = held[half * 2 + a - 1]
                high = source.astype(BF16)
                rest = source - high.astype(F32)
                middle = rest.astype(BF16)
                low = (rest - middle.astype(F32)).astype(BF16)
                parts = jnp.concatenate([high, middle, low], axis=0)
                found = jnp.dot(pick3, parts, preferred_element_type=F32)
            for t in range(Z):
                rows_out[half, t, a * S : (a + 1) * S, :] = found[t * 8 : t * 8 + S, :]
        for k in range(1, Z):
            copy = pltpu.make_async_remote_copy(
                src_ref=rows_out.at[half, z_peers[k - 1]],
                dst_ref=rows_in.at[half, k - 1],
                send_sem=row_send.at[half, k - 1],
                recv_sem=row_recv.at[half, k - 1],
                device_id=z_devices[k - 1],
                device_id_type=MESH,
            )
            copy.start()
            row_copies.append(copy)

    def over_band(buffer, send, recv):
        copies = [
            pltpu.make_async_remote_copy(
                src_ref=buffer.at[x],
                dst_ref=buffer.at[x],
                send_sem=send.at[n],
                recv_sem=recv.at[x],
                device_id=peer,
                device_id_type=MESH,
            )
            for n, peer in enumerate(x_devices)
        ]
        for copy in copies:
            copy.start()
        return copies

    def from_band(buffer, send, recv):
        for t in x_peers:
            pltpu.make_async_remote_copy(
                src_ref=buffer.at[t],
                dst_ref=buffer.at[t],
                send_sem=send.at[0],
                recv_sem=recv.at[t],
                device_id=everyone[0],
                device_id_type=MESH,
            ).wait_recv()

    band_copies = []

    def arrived(half):
        rows = rows_out[half, z]
        for k in range(1, Z):
            row_copies[half * (Z - 1) + k - 1].wait_recv()
            rows = rows + rows_in[half, k - 1]
        rows_all[half, x] = rows
        band_copies.extend(over_band(rows_all.at[half], all_send.at[half], all_recv.at[half]))

    band_col = lax.broadcasted_iota(jnp.int32, (BD, 1), 0)

    def own_value(ref, m, b):
        value = ref[m, b]
        for xx in range(1, X):
            value = jnp.where(x == xx, ref[m, xx * BD + b], value)
        return value

    def own_column(ref, m):
        column = jnp.zeros((BD, 1), F32)
        for b in range(BD):
            column = jnp.where(band_col == b, own_value(ref, m, b), column)
        return column

    share_cols = [own_column(share_ref, m) for m in range(NM)]
    emis_cols = [own_column(emis_ref, k) for k in range(NCLS)]
    arrived(0)
    from_band(rows_all.at[0], all_send.at[0], all_recv.at[0])
    weights, emis_slots = [], []
    for n in range(slots):
        xx, s = n // S, n % S
        ids = rows_all[0, xx, s : s + 1, :]
        emis = jnp.broadcast_to(emis_cols[0], (BD, FG))
        material = ids
        for k in range(1, NCLS):
            emis = jnp.where(ids > k * NM - 0.5, emis_cols[k], emis)
            material = jnp.where(ids > k * NM - 0.5, ids - k * NM, material)
        share = jnp.broadcast_to(share_cols[0], (BD, FG))
        for m in range(1, NM):
            share = jnp.where(material > m - 0.5, share_cols[m], share)
        weight = emis * share
        weights.append(weight)
        emis_slots.append(emis)
        rad[n] = weight * rows_all[0, xx, S + s : S + s + 1, :]
    load_kern.wait()

    def block_of(zz, cc):
        return zz * C + cc

    totals = []
    for k in range(NCLS):
        for m in range(NM):
            total = emis_ref[k, 0] * share_ref[m, 0]
            for b in range(1, NB):
                total = total + emis_ref[k, b] * share_ref[m, b]
            totals.append(total)

    def emit_of(ids):
        emit_sum = jnp.full(ids.shape, totals[0], F32)
        for n in range(1, len(totals)):
            emit_sum = jnp.where(ids > n - 0.5, totals[n], emit_sum)
        return emit_sum

    rows_block = slots * BD
    for sweep in range(SWEEPS):
        mine = block_of(z, c)
        started = []
        final = sweep == SWEEPS - 1
        buffer = last if final else gath.at[sweep]

        def send(block, peer):
            copy = pltpu.make_async_remote_copy(
                src_ref=buffer.at[block],
                dst_ref=buffer.at[block],
                send_sem=send_sem.at[sweep, len(started)],
                recv_sem=recv_sem.at[sweep, block],
                device_id=peer,
                device_id_type=pl.DeviceIdType.MESH,
            )
            copy.start()
            started.append(copy)

        def receive(block):
            pltpu.make_async_remote_copy(
                src_ref=buffer.at[block],
                dst_ref=buffer.at[block],
                send_sem=send_sem.at[sweep, 0],
                recv_sem=recv_sem.at[sweep, block],
                device_id=everyone[0],
                device_id_type=pl.DeviceIdType.MESH,
            ).wait_recv()

        for n in range(slots):
            xx, end, q = n // S, n % S // ppd, n % ppd
            pair = kern[xx * ppd + q]
            if end == 0:
                term = lax.dot_general(
                    rad[n + ppd].astype(BF16), pair, (((1,), (1,)), ((), ())), preferred_element_type=F32
                )
            else:
                term = jnp.dot(rad[n - ppd].astype(BF16), pair, preferred_element_type=F32)
            stage[n * BD : (n + 1) * BD, :] = term
        buffer[mine] = stage[...].astype(buffer.dtype)

        for peer in z_devices + c_devices:
            send(mine, peer)
        if not final:
            arrived(1)
            emit_rows = [emit_of(rows_all[0, xx, :S, :]) for xx in range(X)]
            emit_sums = [emit_rows[n // S][n % S : n % S + 1, :] for n in range(slots)]
            from_band(rows_all.at[1], all_send.at[1], all_recv.at[1])
        else:
            emit_held[...] = emit_of(ident[...])
            emis_held = []
            for b in range(BD):
                emis = jnp.full(coat.shape, own_value(emis_ref, 0, b), F32)
                for k in range(1, NCLS):
                    emis = jnp.where(coat == k, own_value(emis_ref, k, b), emis)
                emis_held.append(emis)
                share = jnp.full(mats.shape, own_value(share_ref, 0, b), F32)
                for m in range(1, NM):
                    share = jnp.where(mats[...] == m, own_value(share_ref, m, b), share)
                weight_held[b] = emis * share
        for zt in z_peers:
            receive(block_of(zt, c))
            for peer in c_devices:
                send(block_of(zt, c), peer)
        for ct in c_peers:
            for zt in [z] + z_peers:
                receive(block_of(zt, ct))

        if sweep == 0:
            for t in z_peers + [z]:
                for u in c_peers:
                    info_copy(0, t * C + u, everyone[0]).wait_recv()
            tiles = []
            for t in range(Z * C // per_tile):
                tile = info[t * per_tile]
                for n in range(1, per_tile):
                    tile = tile + info[t * per_tile + n]
                tiles.append(tile[7:8, :])
            key_row = jnp.concatenate(tiles, axis=1)

        terms = buffer[...].reshape(-1, FG)
        count = terms.shape[0]
        if not final:
            select = jnp.where(own_key[:, :1] == key_row, jnp.ones((rows_block, count), F32), 0.0)
            incoming = jnp.dot(select.astype(BF16), terms, preferred_element_type=F32)
            stage[...] = incoming
            for n in range(slots):
                xx, s = n // S, n % S
                irradiance = stage[n * BD : (n + 1) * BD, :] / rows_all[1, xx, s : s + 1, :]
                stage[n * BD : (n + 1) * BD, :] = irradiance
                sum_first[x, n : n + 1, :] = jnp.sum(emis_slots[n] * irradiance, axis=0, keepdims=True)
            band_copies.extend(over_band(sum_first, sum_send.at[0], sum_recv.at[0]))
            from_band(sum_first, sum_send.at[0], sum_recv.at[0])
            absorbed = sum_first[0]
            for xx in range(1, X):
                absorbed = absorbed + sum_first[xx]
            for n in range(slots):
                xx, s = n // S, n % S
                fourth = (absorbed[n : n + 1, :] + rows_all[1, xx, S + s : S + s + 1, :]) / emit_sums[n]
                irradiance = stage[n * BD : (n + 1) * BD, :]
                rad[n] = weights[n] * fourth + (1.0 - emis_slots[n]) * irradiance
        else:
            out_row = lax.broadcasted_iota(jnp.int32, (BD * groups_dev, count), 0)
            row_key = (out_row % groups_dev + z * groups_dev) * BD + out_row // groups_dev
            select = jnp.where(row_key == key_row, jnp.ones(row_key.shape, F32), 0.0).astype(BF16)
            high = terms.astype(BF16)
            low = (terms - high.astype(F32)).astype(BF16)
            inc_all[...] = jnp.dot(select, high, preferred_element_type=F32) + jnp.dot(
                select, low, preferred_element_type=F32
            )
            partial = jnp.zeros((groups_dev, FG), F32)
            for b in range(BD):
                irradiance = inc_all[b * groups_dev : (b + 1) * groups_dev, :] / held[1]
                inc_all[b * groups_dev : (b + 1) * groups_dev, :] = irradiance
                partial = partial + emis_held[b] * irradiance
            sum_last[x] = partial
            band_copies.extend(over_band(sum_last, sum_send.at[1], sum_recv.at[1]))
            from_band(sum_last, sum_send.at[1], sum_recv.at[1])
            absorbed = sum_last[0]
            for xx in range(1, X):
                absorbed = absorbed + sum_last[xx]
            fourth = (absorbed + held[2]) / emit_held[...]
            fourth_ref[...] = fourth
            for b in range(BD):
                irradiance = inc_all[b * groups_dev : (b + 1) * groups_dev, :]
                result = weight_held[b] * fourth + (1.0 - emis_held[b]) * irradiance
                out_ref[b] = result.astype(BF16)
        for copy in started:
            copy.wait_send()
    for copy in info_copies + row_copies + band_copies:
        copy.wait_send()


def on_device(
    pair_list, kernel, facet_areas, heat_load, start_t4, material, coating, emis_table, share_table
):
    groups_dev, FG = facet_areas.shape
    NCLS, NB = emis_table.shape
    NM = share_table.shape[0]
    Z, X, C = lax.axis_size("grp"), lax.axis_size("band"), lax.axis_size("half")
    pairs_dev = pair_list.shape[0]
    ppd = pairs_dev // X
    S = 2 * ppd
    D = Z * C
    bands_dev = NB // X

    smem = pl.BlockSpec(memory_space=pltpu.SMEM)
    dma = pltpu.SemaphoreType.DMA
    radiosity, fourth = pl.pallas_call(
        functools.partial(exchange, (Z, X, C, S, ppd, NB, NM, NCLS)),
        out_shape=(
            jax.ShapeDtypeStruct((bands_dev, groups_dev, FG), BF16),
            jax.ShapeDtypeStruct((groups_dev, FG), F32),
        ),
        in_specs=[smem] * 4 + [pl.BlockSpec(memory_space=pl.ANY)] * 5,
        out_specs=(pl.BlockSpec(memory_space=pltpu.VMEM),) * 2,
        scratch_shapes=[
            pltpu.VMEM((3, groups_dev, FG), F32),
            pltpu.VMEM((groups_dev, FG), jnp.int32),
            pltpu.VMEM((groups_dev, FG), F32),
            pltpu.VMEM((pairs_dev, FG, FG), BF16),
            pltpu.VMEM((Z * C, 8, 128), jnp.int32),
            pltpu.VMEM((2, Z, 2 * S, FG), F32),
            pltpu.VMEM((2, Z - 1, 2 * S, FG), F32),
            pltpu.VMEM((2, X, 2 * S, FG), F32),
            pltpu.VMEM((2 * pairs_dev, bands_dev, FG), F32),
            pltpu.VMEM((2 * pairs_dev * bands_dev, FG), F32),
            pltpu.VMEM((SWEEPS - 1, D, 2 * pairs_dev * bands_dev, FG), BF16),
            pltpu.VMEM((D, 2 * pairs_dev * bands_dev, FG), F32),
            pltpu.VMEM((X, 2 * pairs_dev, FG), F32),
            pltpu.VMEM((X, groups_dev, FG), F32),
            pltpu.VMEM((groups_dev, FG), F32),
            pltpu.VMEM((groups_dev * bands_dev, FG), F32),
            pltpu.VMEM((bands_dev, groups_dev, FG), F32),
            dma((3,)),
            dma(()),
            dma(()),
            dma((Z * C,)),
            dma((Z * C,)),
            dma((2, Z - 1)),
            dma((2, Z - 1)),
            dma((2, X - 1)),
            dma((2, X)),
            dma((2, X - 1)),
            dma((2, X)),
            dma((SWEEPS, 2 * D)),
            dma((SWEEPS, D)),
        ],
        compiler_params=pltpu.CompilerParams(
            collective_id=0, has_side_effects=True, vmem_limit_bytes=60 * 1024 * 1024
        ),
        cost_estimate=pl.CostEstimate(flops=200_000_000, bytes_accessed=8_000_000, transcendentals=0),
    )(
        pair_list, coating, emis_table, share_table,
        material, start_t4, facet_areas, heat_load, kernel,
    )

    return (radiosity.transpose(1, 0, 2), fourth**0.25)


def solution(mesh):
    return jax.shard_map(
        on_device,
        mesh=mesh,
        in_specs=(
            P(("parts", "grp", "half"), None),
            P(("parts", "grp", "half"), None, None),
            P(("parts", "grp"), None),
            P(("parts", "grp"), None),
            P(("parts", "grp"), None),
            P(("parts", "grp"), None),
            P(("parts", "grp")),
            P(),
            P(),
        ),
        out_specs=(P(("parts", "grp"), "band", None), P(("parts", "grp"), None)),
        check_vma=False,
    )
```

```python
import functools

import jax
import jax.numpy as jnp
from jax import lax
from jax.experimental import pallas as pl
from jax.experimental.pallas import tpu as pltpu
from jax.sharding import PartitionSpec as P

SWEEPS = 2
F32 = jnp.float32
BF16 = jnp.bfloat16


def exchange(kernel_dims, *refs):
    Z, X, C, S, ppd, NB, NM, NCLS = kernel_dims
    slots, BD = X * S, NB // X
    (
        pair_ref, coat_ref, emis_ref, share_ref,
        mat_hbm, start_hbm, areas_hbm, heat_hbm, kern_hbm, out_ref, fourth_ref,
        held, mats, ident, kern, info, rows_out, rows_in, rows_all, rad, stage, gath, last, sum_first, sum_last, emit_held, inc_all, weight_held,
        held_sem, mat_sem, kern_sem, info_send, info_recv, row_send, row_recv,
        all_send, all_recv, sum_send, sum_recv, send_sem, recv_sem,
    ) = refs
    z, x, c = lax.axis_index("grp"), lax.axis_index("band"), lax.axis_index("half")
    groups_dev, FG = mats.shape
    MESH = pl.DeviceIdType.MESH

    loads = [
        pltpu.make_async_copy(source, held.at[a], held_sem.at[a])
        for a, source in enumerate((start_hbm, areas_hbm, heat_hbm))
    ]
    loads.insert(0, pltpu.make_async_copy(mat_hbm, mats, mat_sem))
    for load in loads:
        load.start()
    load_kern = pltpu.make_async_copy(kern_hbm, kern, kern_sem)
    load_kern.start()

    barrier = pltpu.get_barrier_semaphore()
    z_peers = [lax.rem(z + k, Z) for k in range(1, Z)]
    x_peers = [lax.rem(x + k, X) for k in range(1, X)]
    c_peers = [lax.rem(c + k, C) for k in range(1, C)]
    z_devices = [{"grp": t} for t in z_peers]
    x_devices = [{"band": t} for t in x_peers]
    c_devices = [{"half": t} for t in c_peers]
    far_devices = [{"grp": t, "half": u} for t in z_peers for u in c_peers]
    everyone = z_devices + c_devices + far_devices + x_devices
    for peer in everyone:
        pl.semaphore_signal(barrier, inc=1, device_id=peer, device_id_type=MESH)

    width = slots * BD
    per_tile = 128 // width
    mine_info = z * C + c
    lane = lax.broadcasted_iota(jnp.int32, (8, 128), 1)
    row = lax.broadcasted_iota(jnp.int32, (8, 128), 0)
    first_lane = lax.rem(mine_info, per_tile) * width
    slot_at = lane // BD - first_lane // BD
    keys = jnp.zeros((8, 128), jnp.int32)
    for xx in range(X):
        for s in range(S):
            group = pair_ref[xx * ppd + s % ppd, s // ppd]
            keys = jnp.where(slot_at == xx * S + s, group * BD + lane % BD, keys)
    columns = jnp.full((8, 128), -1, jnp.int32)
    band_of = lax.broadcasted_iota(jnp.int32, (slots * BD, 128), 0)
    own_key = jnp.zeros((slots * BD, 128), jnp.int32)
    for s in range(S):
        group = jnp.int32(0)
        for xx in range(X):
            here = pair_ref[xx * ppd + s % ppd, s // ppd]
            group = jnp.where(x == xx, here, group)
            own_key = jnp.where(band_of // BD == xx * S + s, here * BD + band_of % BD, own_key)
        columns = jnp.where(row == s, group, columns)
    info[mine_info] = jnp.where(row == 7, keys, columns)

    pl.semaphore_wait(barrier, len(everyone))

    def info_copy(n, block, peer):
        return pltpu.make_async_remote_copy(
            src_ref=info.at[block],
            dst_ref=info.at[block],
            send_sem=info_send.at[n],
            recv_sem=info_recv.at[block],
            device_id=peer,
            device_id_type=MESH,
        )

    info_copies = []
    for n, peer in enumerate(z_devices + c_devices + far_devices):
        copy = info_copy(n, mine_info, peer)
        copy.start()
        info_copies.append(copy)
    coat = jnp.zeros((groups_dev, 1), jnp.int32)
    group_row = lax.broadcasted_iota(jnp.int32, (groups_dev, 1), 0)
    for g in range(groups_dev):
        coat = jnp.where(group_row == g, coat_ref[g], coat)
    for load in loads:
        load.wait()
    ident[...] = (coat * NM + mats[...]).astype(F32)
    for t in z_peers:
        info_copy(0, t * C + c, everyone[0]).wait_recv()

    want = jnp.concatenate([info[t * C + c] for t in range(Z)], axis=0)[:, :groups_dev]
    local = lax.broadcasted_iota(jnp.int32, (Z * 8, groups_dev), 1) + z * groups_dev
    pick = jnp.where(want == local, jnp.ones(want.shape, F32), 0.0)
    pick3 = jnp.concatenate([pick] * 3, axis=1).astype(BF16)
    pick = pick.astype(BF16)
    row_copies = []
    for half in range(2):
        for a in range(2):
            if half + a == 0:
                found = jnp.dot(pick, ident[...].astype(BF16), preferred_element_type=F32)
            else:
                source = held[half * 2 + a - 1]
                high = source.astype(BF16)
                rest = source - high.astype(F32)
                middle = rest.astype(BF16)
                low = (rest - middle.astype(F32)).astype(BF16)
                parts = jnp.concatenate([high, middle, low], axis=0)
                found = jnp.dot(pick3, parts, preferred_element_type=F32)
            for t in range(Z):
                rows_out[half, t, a * S : (a + 1) * S, :] = found[t * 8 : t * 8 + S, :]
        for k in range(1, Z):
            copy = pltpu.make_async_remote_copy(
                src_ref=rows_out.at[half, z_peers[k - 1]],
                dst_ref=rows_in.at[half, k - 1],
                send_sem=row_send.at[half, k - 1],
                recv_sem=row_recv.at[half, k - 1],
                device_id=z_devices[k - 1],
                device_id_type=MESH,
            )
            copy.start()
            row_copies.append(copy)

    def over_band(buffer, send, recv):
        copies = [
            pltpu.make_async_remote_copy(
                src_ref=buffer.at[x],
                dst_ref=buffer.at[x],
                send_sem=send.at[n],
                recv_sem=recv.at[x],
                device_id=peer,
                device_id_type=MESH,
            )
            for n, peer in enumerate(x_devices)
        ]
        for copy in copies:
            copy.start()
        return copies

    def from_band(buffer, send, recv):
        for t in x_peers:
            pltpu.make_async_remote_copy(
                src_ref=buffer.at[t],
                dst_ref=buffer.at[t],
                send_sem=send.at[0],
                recv_sem=recv.at[t],
                device_id=everyone[0],
                device_id_type=MESH,
            ).wait_recv()

    band_copies = []

    def arrived(half):
        rows = rows_out[half, z]
        for k in range(1, Z):
            row_copies[half * (Z - 1) + k - 1].wait_recv()
            rows = rows + rows_in[half, k - 1]
        rows_all[half, x] = rows
        band_copies.extend(over_band(rows_all.at[half], all_send.at[half], all_recv.at[half]))

    band_col = lax.broadcasted_iota(jnp.int32, (BD, 1), 0)

    def own_value(ref, m, b):
        value = ref[m, b]
        for xx in range(1, X):
            value = jnp.where(x == xx, ref[m, xx * BD + b], value)
        return value

    def own_column(ref, m):
        column = jnp.zeros((BD, 1), F32)
        for b in range(BD):
            column = jnp.where(band_col == b, own_value(ref, m, b), column)
        return column

    share_cols = [own_column(share_ref, m) for m in range(NM)]
    emis_cols = [own_column(emis_ref, k) for k in range(NCLS)]
    arrived(0)
    from_band(rows_all.at[0], all_send.at[0], all_recv.at[0])
    weights, emis_slots = [], []
    for n in range(slots):
        xx, s = n // S, n % S
        ids = rows_all[0, xx, s : s + 1, :]
        emis = jnp.broadcast_to(emis_cols[0], (BD, FG))
        material = ids
        for k in range(1, NCLS):
            emis = jnp.where(ids > k * NM - 0.5, emis_cols[k], emis)
            material = jnp.where(ids > k * NM - 0.5, ids - k * NM, material)
        share = jnp.broadcast_to(share_cols[0], (BD, FG))
        for m in range(1, NM):
            share = jnp.where(material > m - 0.5, share_cols[m], share)
        weight = emis * share
        weights.append(weight)
        emis_slots.append(emis)
        rad[n] = weight * rows_all[0, xx, S + s : S + s + 1, :]
    load_kern.wait()

    def block_of(zz, cc):
        return zz * C + cc

    totals = []
    for k in range(NCLS):
        for m in range(NM):
            total = emis_ref[k, 0] * share_ref[m, 0]
            for b in range(1, NB):
                total = total + emis_ref[k, b] * share_ref[m, b]
            totals.append(total)

    def emit_of(ids):
        emit_sum = jnp.full(ids.shape, totals[0], F32)
        for n in range(1, len(totals)):
            emit_sum = jnp.where(ids > n - 0.5, totals[n], emit_sum)
        return emit_sum

    rows_block = slots * BD
    for sweep in range(SWEEPS):
        mine = block_of(z, c)
        started = []
        final = sweep == SWEEPS - 1
        buffer = last if final else gath.at[sweep]

        def send(block, peer):
            copy = pltpu.make_async_remote_copy(
                src_ref=buffer.at[block],
                dst_ref=buffer.at[block],
                send_sem=send_sem.at[sweep, len(started)],
                recv_sem=recv_sem.at[sweep, block],
                device_id=peer,
                device_id_type=pl.DeviceIdType.MESH,
            )
            copy.start()
            started.append(copy)

        def receive(block):
            pltpu.make_async_remote_copy(
                src_ref=buffer.at[block],
                dst_ref=buffer.at[block],
                send_sem=send_sem.at[sweep, 0],
                recv_sem=recv_sem.at[sweep, block],
                device_id=everyone[0],
                device_id_type=pl.DeviceIdType.MESH,
            ).wait_recv()

        for n in range(slots):
            xx, end, q = n // S, n % S // ppd, n % ppd
            pair = kern[xx * ppd + q]
            if end == 0:
                term = lax.dot_general(
                    rad[n + ppd].astype(BF16), pair, (((1,), (1,)), ((), ())), preferred_element_type=F32
                )
            else:
                term = jnp.dot(rad[n - ppd].astype(BF16), pair, preferred_element_type=F32)
            stage[n * BD : (n + 1) * BD, :] = term
        buffer[mine] = stage[...].astype(buffer.dtype)

        for peer in z_devices + c_devices:
            send(mine, peer)
        if not final:
            arrived(1)
            emit_rows = [emit_of(rows_all[0, xx, :S, :]) for xx in range(X)]
            emit_sums = [emit_rows[n // S][n % S : n % S + 1, :] for n in range(slots)]
            from_band(rows_all.at[1], all_send.at[1], all_recv.at[1])
        else:
            emit_held[...] = emit_of(ident[...])
            emis_held = []
            for b in range(BD):
                emis = jnp.full(coat.shape, own_value(emis_ref, 0, b), F32)
                for k in range(1, NCLS):
                    emis = jnp.where(coat == k, own_value(emis_ref, k, b), emis)
                emis_held.append(emis)
                share = jnp.full(mats.shape, own_value(share_ref, 0, b), F32)
                for m in range(1, NM):
                    share = jnp.where(mats[...] == m, own_value(share_ref, m, b), share)
                weight_held[b] = emis * share
        for zt in z_peers:
            receive(block_of(zt, c))
            for peer in c_devices:
                send(block_of(zt, c), peer)
        for ct in c_peers:
            for zt in [z] + z_peers:
                receive(block_of(zt, ct))

        if sweep == 0:
            for t in z_peers + [z]:
                for u in c_peers:
                    info_copy(0, t * C + u, everyone[0]).wait_recv()
            tiles = []
            for t in range(Z * C // per_tile):
                tile = info[t * per_tile]
                for n in range(1, per_tile):
                    tile = tile + info[t * per_tile + n]
                tiles.append(tile[7:8, :])
            key_row = jnp.concatenate(tiles, axis=1)

        terms = buffer[...].reshape(-1, FG)
        count = terms.shape[0]
        if not final:
            select = jnp.where(own_key[:, :1] == key_row, jnp.ones((rows_block, count), F32), 0.0)
            incoming = jnp.dot(select.astype(BF16), terms, preferred_element_type=F32)
            stage[...] = incoming
            for n in range(slots):
                xx, s = n // S, n % S
                irradiance = stage[n * BD : (n + 1) * BD, :] / rows_all[1, xx, s : s + 1, :]
                stage[n * BD : (n + 1) * BD, :] = irradiance
                sum_first[x, n : n + 1, :] = jnp.sum(emis_slots[n] * irradiance, axis=0, keepdims=True)
            band_copies.extend(over_band(sum_first, sum_send.at[0], sum_recv.at[0]))
            from_band(sum_first, sum_send.at[0], sum_recv.at[0])
            absorbed = sum_first[0]
            for xx in range(1, X):
                absorbed = absorbed + sum_first[xx]
            for n in range(slots):
                xx, s = n // S, n % S
                fourth = (absorbed[n : n + 1, :] + rows_all[1, xx, S + s : S + s + 1, :]) / emit_sums[n]
                irradiance = stage[n * BD : (n + 1) * BD, :]
                rad[n] = weights[n] * fourth + (1.0 - emis_slots[n]) * irradiance
        else:
            out_row = lax.broadcasted_iota(jnp.int32, (BD * groups_dev, count), 0)
            row_key = (out_row % groups_dev + z * groups_dev) * BD + out_row // groups_dev
            select = jnp.where(row_key == key_row, jnp.ones(row_key.shape, F32), 0.0).astype(BF16)
            high = terms.astype(BF16)
            low = (terms - high.astype(F32)).astype(BF16)
            inc_all[...] = jnp.dot(select, high, preferred_element_type=F32) + jnp.dot(
                select, low, preferred_element_type=F32
            )
            partial = jnp.zeros((groups_dev, FG), F32)
            for b in range(BD):
                irradiance = inc_all[b * groups_dev : (b + 1) * groups_dev, :] / held[1]
                inc_all[b * groups_dev : (b + 1) * groups_dev, :] = irradiance
                partial = partial + emis_held[b] * irradiance
            sum_last[x] = partial
            band_copies.extend(over_band(sum_last, sum_send.at[1], sum_recv.at[1]))
            from_band(sum_last, sum_send.at[1], sum_recv.at[1])
            absorbed = sum_last[0]
            for xx in range(1, X):
                absorbed = absorbed + sum_last[xx]
            fourth = (absorbed + held[2]) / emit_held[...]
            fourth_ref[...] = fourth
            for b in range(BD):
                irradiance = inc_all[b * groups_dev : (b + 1) * groups_dev, :]
                result = weight_held[b] * fourth + (1.0 - emis_held[b]) * irradiance
                out_ref[b] = result.astype(BF16)
        for copy in started:
            copy.wait_send()
    for copy in info_copies + row_copies + band_copies:
        copy.wait_send()


def on_device(
    pair_list, kernel, facet_areas, heat_load, start_t4, material, coating, emis_table, share_table
):
    groups_dev, FG = facet_areas.shape
    NCLS, NB = emis_table.shape
    NM = share_table.shape[0]
    Z, X, C = lax.axis_size("grp"), lax.axis_size("band"), lax.axis_size("half")
    pairs_dev = pair_list.shape[0]
    ppd = pairs_dev // X
    S = 2 * ppd
    D = Z * C
    bands_dev = NB // X

    smem = pl.BlockSpec(memory_space=pltpu.SMEM)
    dma = pltpu.SemaphoreType.DMA
    radiosity, fourth = pl.pallas_call(
        functools.partial(exchange, (Z, X, C, S, ppd, NB, NM, NCLS)),
        out_shape=(
            jax.ShapeDtypeStruct((bands_dev, groups_dev, FG), BF16),
            jax.ShapeDtypeStruct((groups_dev, FG), F32),
        ),
        in_specs=[smem] * 4 + [pl.BlockSpec(memory_space=pl.ANY)] * 5,
        out_specs=(pl.BlockSpec(memory_space=pltpu.VMEM),) * 2,
        scratch_shapes=[
            pltpu.VMEM((3, groups_dev, FG), F32),
            pltpu.VMEM((groups_dev, FG), jnp.int32),
            pltpu.VMEM((groups_dev, FG), F32),
            pltpu.VMEM((pairs_dev, FG, FG), BF16),
            pltpu.VMEM((Z * C, 8, 128), jnp.int32),
            pltpu.VMEM((2, Z, 2 * S, FG), F32),
            pltpu.VMEM((2, Z - 1, 2 * S, FG), F32),
            pltpu.VMEM((2, X, 2 * S, FG), F32),
            pltpu.VMEM((2 * pairs_dev, bands_dev, FG), F32),
            pltpu.VMEM((2 * pairs_dev * bands_dev, FG), F32),
            pltpu.VMEM((SWEEPS - 1, D, 2 * pairs_dev * bands_dev, FG), BF16),
            pltpu.VMEM((D, 2 * pairs_dev * bands_dev, FG), F32),
            pltpu.VMEM((X, 2 * pairs_dev, FG), F32),
            pltpu.VMEM((X, groups_dev, FG), F32),
            pltpu.VMEM((groups_dev, FG), F32),
            pltpu.VMEM((groups_dev * bands_dev, FG), F32),
            pltpu.VMEM((bands_dev, groups_dev, FG), F32),
            dma((3,)),
            dma(()),
            dma(()),
            dma((Z * C,)),
            dma((Z * C,)),
            dma((2, Z - 1)),
            dma((2, Z - 1)),
            dma((2, X - 1)),
            dma((2, X)),
            dma((2, X - 1)),
            dma((2, X)),
            dma((SWEEPS, 2 * D)),
            dma((SWEEPS, D)),
        ],
        compiler_params=pltpu.CompilerParams(
            collective_id=0, has_side_effects=True, vmem_limit_bytes=60 * 1024 * 1024
        ),
        cost_estimate=pl.CostEstimate(flops=200_000_000, bytes_accessed=8_000_000, transcendentals=0),
    )(
        pair_list, coating, emis_table, share_table,
        material, start_t4, facet_areas, heat_load, kernel,
    )

    return (radiosity.transpose(1, 0, 2), jnp.sqrt(jnp.sqrt(fourth)))


def solution(mesh):
    return jax.shard_map(
        on_device,
        mesh=mesh,
        in_specs=(
            P(("parts", "grp", "half"), None),
            P(("parts", "grp", "half"), None, None),
            P(("parts", "grp"), None),
            P(("parts", "grp"), None),
            P(("parts", "grp"), None),
            P(("parts", "grp"), None),
            P(("parts", "grp")),
            P(),
            P(),
        ),
        out_specs=(P(("parts", "grp"), "band", None), P(("parts", "grp"), None)),
        check_vma=False,
    )
```
